32 devices in a mesh: rep: 2 (over y), fsdp: 4 (over x, core), patch: 4 (over z).
Axes of the slice: x: 2, y: 2, z: 4, core: 2. Of those that a mesh axis runs over, the one named last changes fastest.
Arguments:
- latent: bfloat16 [4, 512, 6144], P('rep', 'fsdp', 'patch'), parts along dimension 0, may hold values from -3 to 3
- timestep: int32 [4], P('rep'), parts along dimension 0, may hold values from 0 to 49, as said below
- positions: int32 [1024], P(('rep', 'fsdp')), parts along dimension 0, may hold values from 0 to 511, each once
- modulation: bfloat16 [50, 3, 6144], P(None, None, 'patch'), may hold values from -3 to 3
- qkv_weight: bfloat16 [6144, 3, 3072], P('fsdp', None, 'patch'), may hold values from -0.078125 to 0.078125
- out_weight: bfloat16 [3072, 6144], P('patch', 'fsdp'), may hold values from -1.25 to 1.25
- query_gain: float32 [128], replicated, may hold values from 0.1 to 1.9
- key_gain: float32 [128], replicated, may hold values from 0.1 to 1.9
- stale_keys: bfloat16 [4, 512, 3072], P('rep', 'fsdp', 'patch'), parts along dimension 0, may hold values from -140 to 140
- stale_values: bfloat16 [4, 512, 3072], P('rep', 'fsdp', 'patch'), parts along dimension 0, may hold values from -6 to 6
Outputs:
- block_out: bfloat16 [4, 512, 6144], P('rep', 'fsdp', 'patch'), parts along dimension 0
- new_keys: bfloat16 [4, 512, 3072], P('rep', 'fsdp', 'patch'), parts along dimension 0
- new_values: bfloat16 [4, 512, 3072], P('rep', 'fsdp', 'patch'), parts along dimension 0
The draws below stay inside these ranges and needn't reach their ends.
There are 2 independent parts, one for each index of `rep`. The reference program is written for one: setup_inputs(seed, part) draws one part's arguments, and reference() takes and returns one part's arrays. A program takes and returns all parts, laid end to end along the dimension named above; an argument that names none is the same for every part. Nothing has to cross between parts.
Inputs may be any that keep to these rules, and one draw needn't show every extreme that they name: Each of the 512 grid positions appears once. `timestep`: the 2 entries are distinct.
All inputs are finite; a program needn't handle non-finite values.
Results may differ from the reference program's by a relative error of at most 0.012.
The reference program's roundings to bfloat16 on the way (of `picked`, `modded`, `queries`, `probs` and `mixed`) count: a program that leaves them out, or rounds other values in their place, can miss the bound.
Values may be sent and summed in bfloat16 or wider, within the bound.
No kernel may reach another device: no remote copies, remote signals or barrier semaphores. Data moves between devices by JAX's collectives and lax.ppermute only.
A program may use at most 128 MiB of HBM per device.

```python
import jax
import jax.numpy as jnp
from jax import lax

D = 6144
HD = 128
HEADS = 24
GRID_W = 62
STEPS = 50
SEQS = 2
TOK_DEV = 128
TOKENS = 512
N_FSDP = 4
N_PATCH = 4


def draw_timestep(key, part):
    key = jax.random.fold_in(key, 7)
    order = jax.random.permutation(key, STEPS)
    return order[:SEQS].astype(jnp.int32)


def draw_stale_keys(key, part):
    key = jax.random.fold_in(key, 11)
    first = jax.random.fold_in(key, 0)
    shape = (SEQS, TOKENS, HEADS * HD)
    base = jnp.clip(jax.random.normal(first, shape, jnp.float32), -6.0, 6.0)
    return base.astype(jnp.bfloat16)


def block_scale(rng, dims, cuts, smallest, high):
    def one(position, blocks):
        heights = jax.random.uniform(jax.random.fold_in(jax.random.fold_in(rng, 6), position), (blocks,), jnp.float32, smallest / len(cuts), high / len(cuts))
        return jnp.repeat(jnp.exp(heights), dims[position] // blocks).reshape((-1,) + (1,) * (len(dims) - position - 1))

    loudness = one(*cuts[0])
    for cut in cuts[1:]:
        loudness = loudness * one(*cut)
    return loudness


def bell_draw(key, extent, scale, most, cuts=(), kind=jnp.bfloat16):
    array = jax.random.normal(key, extent, jnp.float32) * scale
    if len(cuts) > 0:
        array = block_scale(key, extent, cuts, -0.22, 0.18) * array
    return jnp.clip(array, min=-most, max=most).astype(kind)


def setup_inputs(seed: int = 0, part: int = 0) -> dict:
    key_of = jax.random.split(jax.random.key(seed), 11)
    own_keys = jax.random.split(jax.random.fold_in(key_of[10], part), 11)
    return {
        "latent": bell_draw(own_keys[0], (SEQS, TOKENS, D), 0.5, 3.0, ((1, 4), (2, 4))),
        "timestep": draw_timestep(jax.random.fold_in(jax.random.fold_in(key_of[10], part), 71), part),
        "positions": jax.random.permutation(own_keys[2], TOKENS).astype(jnp.int32),
        "modulation": bell_draw(key_of[3], (STEPS, 3, D), 0.5, 3.0, ((2, 4),)),
        "qkv_weight": bell_draw(key_of[4], (D, 3, HEADS * HD), D ** -0.5, 0.078125, ((0, 4), (2, 4))),
        "out_weight": bell_draw(key_of[5], (HEADS * HD, D), (4 * HEADS * HD // TOKENS) ** -0.5, 1.25, ((0, 4), (1, 4))),
        "query_gain": jnp.clip(1.0 + 0.18 * jax.random.normal(key_of[6], (HD,), jnp.float32), 0.1, 1.9),
        "key_gain": jnp.clip(1.0 + 0.18 * jax.random.normal(key_of[7], (HD,), jnp.float32), 0.1, 1.9),
        "stale_keys": draw_stale_keys(jax.random.fold_in(jax.random.fold_in(key_of[10], part), 71), part),
        "stale_values": bell_draw(own_keys[9], (SEQS, TOKENS, HEADS * HD), 1.0, 6.0, ((1, 4), (2, 4))),
    }


EPS = 1e-06

def norm_heads(values, gain):
    return values * lax.rsqrt(lax.optimization_barrier(jnp.mean(values * values, axis=-1, keepdims=True)) + EPS) * gain

def rotate(values, places):
    quarter = values.shape[-1] // 4
    freq = 10000.0 ** (-jnp.arange(quarter, dtype=jnp.float32) / quarter)
    row_pos = (places // GRID_W).astype(jnp.float32)
    col_pos = (places % GRID_W).astype(jnp.float32)
    pieces = []
    for coords, lower in ((row_pos, 0), (col_pos, 2 * quarter)):
        angle = coords[:, None] * freq[None, :]
        cosine = jnp.cos(angle)[None, :, None, :]
        sine = jnp.sin(angle)[None, :, None, :]
        first = values[..., lower:lower + quarter]
        second = values[..., lower + quarter:lower + 2 * quarter]
        pieces.append(first * cosine - second * sine)
        pieces.append(second * cosine + first * sine)
    return jnp.concatenate(pieces, axis=-1)

def reference(latent, timestep, positions, modulation, qkv_weight, out_weight, query_gain, key_gain, stale_keys, stale_values):
    picked = modulation[timestep].astype(jnp.float32)
    shift = picked[:, 0][:, None, :]
    scale = picked[:, 1][:, None, :]
    gate = picked[:, 2][:, None, :]
    values = latent.astype(jnp.float32)
    mean = lax.optimization_barrier(jnp.mean(values, axis=-1, keepdims=True))
    centered = values - mean
    spread = lax.optimization_barrier(jnp.mean(centered * centered, axis=-1, keepdims=True))
    modded = (centered * lax.rsqrt(spread + EPS) * (1.0 + scale) + shift).astype(jnp.bfloat16)
    width = HEADS * HD
    projected = jnp.dot(modded.reshape(SEQS * TOKENS, D), qkv_weight.reshape(D, 3 * width), preferred_element_type=jnp.float32)
    projected = projected.reshape(SEQS, TOKENS, 3, HEADS, HD)
    queries = rotate(norm_heads(projected[:, :, 0], query_gain), positions).astype(jnp.bfloat16)
    fresh_keys = rotate(norm_heads(projected[:, :, 1], key_gain), positions).astype(jnp.bfloat16)
    fresh_values = projected[:, :, 2].astype(jnp.bfloat16)
    old_keys = stale_keys.reshape(SEQS, TOKENS, HEADS, HD)
    old_values = stale_values.reshape(SEQS, TOKENS, HEADS, HD)
    owner = jnp.arange(TOKENS, dtype=jnp.int32) // TOK_DEV
    factor = 1.0 / HD ** 0.5

    def one_slab(slab):
        own = (owner == slab)[None, :, None, None]
        keys = jnp.where(own, fresh_keys, old_keys).astype(jnp.float32)
        vals = jnp.where(own, fresh_values, old_values).astype(jnp.float32)
        query_rows = lax.dynamic_slice_in_dim(queries, slab * TOK_DEV, TOK_DEV, 1).astype(jnp.float32)
        scores = jnp.einsum('sqhd,skhd->shqk', query_rows, keys) * factor
        top = lax.optimization_barrier(jnp.max(scores, axis=-1, keepdims=True))
        weights = jnp.exp(scores - top)
        total = lax.optimization_barrier(jnp.sum(weights, axis=-1))
        probs = lax.optimization_barrier(weights.astype(jnp.bfloat16)).astype(jnp.float32)
        summed = jnp.einsum('shqk,skhd->shqd', probs, vals)
        result = summed / total[..., None]
        return result.transpose(0, 2, 1, 3).reshape(SEQS, TOK_DEV, width).astype(jnp.bfloat16)
    blocks = lax.map(one_slab, jnp.arange(N_FSDP, dtype=jnp.int32))
    mixed = blocks.transpose(1, 0, 2, 3).reshape(SEQS * TOKENS, width)
    group = width // N_PATCH
    attended = jnp.zeros((SEQS * TOKENS, D), jnp.float32)
    for index in range(N_PATCH):
        term = jnp.dot(mixed[:, index * group:(index + 1) * group], out_weight[index * group:(index + 1) * group], preferred_element_type=jnp.float32)
        attended = attended + lax.optimization_barrier(term.astype(jnp.bfloat16)).astype(jnp.float32)
    attended = attended.reshape(SEQS, TOKENS, D)
    block_out = (values + gate * attended).astype(jnp.bfloat16)
    return (block_out, fresh_keys.reshape(SEQS, TOKENS, width), fresh_values.reshape(SEQS, TOKENS, width))
```

```python
import functools

import jax
import jax.numpy as jnp
from jax import lax
from jax.experimental import pallas as pl
from jax.experimental.pallas import tpu as pltpu
from jax.sharding import PartitionSpec as P

GRID_W = 62


EPS = 1e-06


def norm_heads(values, gain):
    return values * lax.rsqrt(jnp.mean(values * values, axis=-1, keepdims=True) + EPS) * gain


def rotate(values, places):
    quarter = values.shape[-1] // 4
    freq = 10000.0 ** (-jnp.arange(quarter, dtype=jnp.float32) / quarter)
    row_pos = (places // GRID_W).astype(jnp.float32)
    col_pos = (places % GRID_W).astype(jnp.float32)
    pieces = []
    for coords, lower in ((row_pos, 0), (col_pos, 2 * quarter)):
        angle = coords[:, None] * freq[None, :]
        cosine = jnp.cos(angle)[None, :, None, :]
        sine = jnp.sin(angle)[None, :, None, :]
        first = values[..., lower : lower + quarter]
        second = values[..., lower + quarter : lower + 2 * quarter]
        pieces.append(first * cosine - second * sine)
        pieces.append(second * cosine + first * sine)
    return jnp.concatenate(pieces, axis=-1)


def pick_rows(timestep, modulation):
    levels = modulation.shape[0]
    onehot = (timestep[:, None] == jnp.arange(levels, dtype=jnp.int32)[None, :]).astype(
        jnp.bfloat16
    )
    return jnp.einsum(
        "st,tcf->scf", onehot, modulation, preferred_element_type=jnp.float32
    ).astype(jnp.bfloat16)


def shards_any(
    latent,
    timestep,
    positions,
    modulation,
    qkv_weight,
    out_weight,
    query_gain,
    key_gain,
    stale_keys,
    stale_values,
):
    samples, rows, part_width = latent.shape
    head_size = query_gain.shape[0]
    local_width = qkv_weight.shape[2]
    heads = local_width // head_size
    mine = lax.axis_index("fsdp")
    factor = 1.0 / head_size**0.5
    picked = pick_rows(timestep, modulation)
    gate = picked[:, 2, :].astype(jnp.float32)[:, None, :]
    whole, mod_whole = (
        lax.all_gather(latent, "patch", axis=2, tiled=True),
        lax.all_gather(picked, "patch", axis=2, tiled=True),
    )
    values = whole.astype(jnp.float32)
    mean = jnp.mean(values, axis=-1, keepdims=True)
    centered = values - mean
    spread = jnp.mean(centered * centered, axis=-1, keepdims=True)
    shift = mod_whole[:, 0].astype(jnp.float32)[:, None, :]
    scale = mod_whole[:, 1].astype(jnp.float32)[:, None, :]
    modded = (centered * lax.rsqrt(spread + EPS) * (1.0 + scale) + shift).astype(jnp.bfloat16)
    projected = jnp.einsum(
        "std,dch->stch",
        modded,
        lax.all_gather(qkv_weight, "fsdp", axis=0, tiled=True),
        preferred_element_type=jnp.float32,
    )
    queries = rotate(
        norm_heads(projected[:, :, 0].reshape(samples, rows, heads, head_size), query_gain),
        positions,
    ).astype(jnp.bfloat16)
    fresh_keys = rotate(
        norm_heads(projected[:, :, 1].reshape(samples, rows, heads, head_size), key_gain), positions
    ).astype(jnp.bfloat16)
    fresh_flat = projected[:, :, 2].astype(jnp.bfloat16)
    fresh_values = fresh_flat.reshape(samples, rows, heads, head_size)
    scores = (
        jnp.einsum("sqhd,skhd->shqk", queries, fresh_keys, preferred_element_type=jnp.float32)
        * factor
    )
    top = jnp.max(scores, axis=-1)
    weights = jnp.exp(scores - top[..., None])
    total = jnp.sum(weights, axis=-1)
    summed = jnp.einsum(
        "shqk,skhd->shqd",
        weights.astype(jnp.bfloat16),
        fresh_values,
        preferred_element_type=jnp.float32,
    )
    own_low = mine * rows
    run_total = total
    run_sum = summed
    key_piece = lax.all_gather(stale_keys, "fsdp", axis=1, tiled=True).reshape(
        samples, -1, heads, head_size
    )
    value_piece = lax.all_gather(stale_values, "fsdp", axis=1, tiled=True).reshape(
        samples, -1, heads, head_size
    )
    count = key_piece.shape[1]
    piece_scores = (
        jnp.einsum("sqhd,skhd->shqk", queries, key_piece, preferred_element_type=jnp.float32)
        * factor
    )
    index = jnp.arange(count, dtype=jnp.int32)
    skipped = (index >= own_low) & (index < own_low + rows)
    piece_scores = jnp.where(skipped[None, None, None, :], -1e30, piece_scores)
    new_top = jnp.maximum(top, jnp.max(piece_scores, axis=-1))
    piece_weights = jnp.exp(piece_scores - new_top[..., None])
    fade = jnp.exp(top - new_top)
    run_total = run_total * fade + jnp.sum(piece_weights, axis=-1)
    run_sum = run_sum * fade[..., None] + jnp.einsum(
        "shqk,skhd->shqd",
        piece_weights.astype(jnp.bfloat16),
        value_piece,
        preferred_element_type=jnp.float32,
    )
    mixed = (
        (run_sum / run_total[..., None])
        .transpose(0, 2, 1, 3)
        .reshape(samples, rows, local_width)
        .astype(jnp.bfloat16)
    )
    terms = jnp.einsum(
        "sth,hn->stn",
        mixed,
        lax.all_gather(out_weight, "fsdp", axis=1, tiled=True),
        preferred_element_type=jnp.float32,
    )
    attended = lax.psum_scatter(
        terms.astype(jnp.bfloat16), "patch", scatter_dimension=2, tiled=True
    ).astype(jnp.float32)
    block_out = (latent.astype(jnp.float32) + gate * attended).astype(jnp.bfloat16)
    return (block_out, fresh_keys.reshape(samples, rows, local_width), fresh_flat)


def norm_kernel(key, own, one, two, three, turns, *rest):
    outs, held = rest[:4], rest[4]
    blocks = (own, one, two, three)
    width = 4 * own.shape[1]
    mean = sum(jnp.sum(b[...].astype(jnp.float32), axis=-1, keepdims=True) for b in blocks) / width
    spread = (
        sum(
            jnp.sum(jnp.square(b[...].astype(jnp.float32) - mean), axis=-1, keepdims=True)
            for b in blocks
        )
        / width
    )
    rate = lax.rsqrt(spread + EPS)
    for r, block in enumerate(blocks):
        shift = turns[r, 0:1].astype(jnp.float32)
        scale = turns[r, 1:2].astype(jnp.float32)
        centered = block[...].astype(jnp.float32) - mean
        held[r ^ key[0]] = (centered * rate * (1.0 + scale) + shift).astype(jnp.bfloat16)
    for j in range(4):
        outs[j][...] = held[j]


def project_kernel(own, pair, over, cross, weight, kept, sent):
    rows = own.shape[0]
    every = jnp.concatenate([own[...], over[...], pair[...], cross[...]], axis=0)
    product = jnp.dot(every, weight[0], preferred_element_type=jnp.float32)
    for i in range(2):
        kept[i] = product[i * rows : (i + 1) * rows]
        sent[i] = product[(i + 2) * rows : (i + 3) * rows]


def attend_kernel(
    at, kept, back, over, s_pair, s_x, s_d, tables, gains,
    o_own, o_pair, o_x, o_xo, o_d, o_do,
    keys_out, values_out, near, far, mixed, held,
):
    rows, width = keys_out.shape
    size = gains.shape[1]
    half = mixed.shape[2]
    factor = 1.0 / size**0.5
    lane = lax.broadcasted_iota(jnp.int32, (rows, size), 1)
    low = (lane // (size // 4)) % 2 == 0

    def summed(first):
        cols = slice(first, first + size)
        return kept[0, :, cols] + back[0, :, cols] + over[:, cols].astype(jnp.float32)

    def turned(values, gain):
        values = values * lax.rsqrt(jnp.mean(values * values, axis=-1, keepdims=True) + EPS) * gain
        other = jnp.where(
            low, pltpu.roll(values, size - size // 4, 1), pltpu.roll(values, size // 4, 1)
        )
        return (values * tables[0] + other * tables[1]).astype(jnp.bfloat16)

    for h in range(width // size):
        cols = slice(h * size, (h + 1) * size)
        query = turned(summed(h * size), gains[0:1])
        key = turned(summed(width + h * size), gains[1:2])
        value = summed(2 * width + h * size).astype(jnp.bfloat16)
        keys_out[:, cols] = key
        values_out[:, cols] = value
        keys = jnp.concatenate([key] + [s[0, 0, :, cols] for s in (s_pair, s_x, s_d)], axis=0)
        seen = jnp.concatenate([value] + [s[1, 0, :, cols] for s in (s_pair, s_x, s_d)], axis=0)
        scores = (
            lax.dot_general(
                query, keys, (((1,), (1,)), ((), ())), preferred_element_type=jnp.float32
            )
            * factor
        )
        weights = jnp.exp(scores - jnp.max(scores, axis=-1, keepdims=True))
        total = jnp.sum(weights, axis=-1, keepdims=True)
        product = jnp.dot(weights.astype(jnp.bfloat16), seen, preferred_element_type=jnp.float32)
        place = h * size // half
        start = h * size - place * half
        mixed[place, :, start : start + size] = (product / total).astype(jnp.bfloat16)

    rep = at[1]
    for j, (first, second, one, two) in enumerate(
        (
            (o_own, o_own, 0, 1),
            (o_pair, o_pair, 0, 1),
            (o_x, o_xo, rep, 1 - rep),
            (o_d, o_do, rep, 1 - rep),
        )
    ):
        top = first[:half] if first.shape[0] == 2 * half else first[...]
        low_rows = second[half:] if second.shape[0] == 2 * half else second[...]
        term = jnp.dot(mixed[one], top, preferred_element_type=jnp.float32) + jnp.dot(
            mixed[two], low_rows, preferred_element_type=jnp.float32
        )
        held[j ^ at[0]] = term.astype(jnp.bfloat16)
    for i in range(2):
        near[i] = held[2 * i]
        far[i] = held[2 * i + 1]


LIMIT = 56 * 1024 * 1024


def params():
    return pltpu.CompilerParams(vmem_limit_bytes=LIMIT)


def run_norm(key, blocks, turns):
    rows, cols = blocks[0].shape
    vmem = pl.BlockSpec(memory_space=pltpu.VMEM)
    shape = jax.ShapeDtypeStruct((rows, cols), jnp.bfloat16)
    return pl.pallas_call(
        norm_kernel,
        in_specs=[pl.BlockSpec(memory_space=pltpu.SMEM)] + [vmem] * 5,
        out_specs=[vmem] * 4,
        out_shape=[shape] * 4,
        scratch_shapes=[pltpu.VMEM((4, rows, cols), jnp.bfloat16)],
        compiler_params=params(),
        cost_estimate=pl.CostEstimate(
            flops=60 * rows * cols, bytes_accessed=16 * rows * cols, transcendentals=0
        ),
        name="norm",
    )(key, *blocks, turns)


def run_project(own, pair, over, cross, weight):
    rows, depth = own.shape
    wide = weight.shape[2]
    vmem = pl.BlockSpec((rows, depth), lambda i: (0, 0))
    out = pl.BlockSpec((2, rows, wide), lambda i: (0, 0, i))
    shape = jax.ShapeDtypeStruct((2, rows, 3 * wide), jnp.float32)
    return pl.pallas_call(
        project_kernel,
        grid=(3,),
        in_specs=[vmem] * 4 + [pl.BlockSpec((1, depth, wide), lambda i: (i, 0, 0))],
        out_specs=[out, out],
        out_shape=[shape, shape],
        compiler_params=params(),
        cost_estimate=pl.CostEstimate(
            flops=24 * rows * depth * wide,
            bytes_accessed=6 * depth * wide + 48 * rows * wide,
            transcendentals=0,
        ),
        name="project",
    )(own, pair, over, cross, weight)


def run_attend(s, at, kept, back, over, stale, tables, gains, columns):
    rows, triple = over.shape
    width = triple // 3
    feats = columns[0].shape[1]
    full = pl.BlockSpec(memory_space=pltpu.VMEM)
    first = pl.BlockSpec((1, rows, triple), lambda i, at: (0, 0, 0))
    seen = pl.BlockSpec((2, 1, rows, width), lambda i, at: (0, s, 0, 0))
    head = jax.ShapeDtypeStruct((rows, width), jnp.bfloat16)
    term = jax.ShapeDtypeStruct((2, rows, feats), jnp.bfloat16)
    return pl.pallas_call(
        attend_kernel,
        grid_spec=pltpu.PrefetchScalarGridSpec(
            num_scalar_prefetch=1,
            grid=(1,),
            in_specs=[first, first, full] + [seen] * 3 + [full] * 8,
            out_specs=[full] * 4,
            scratch_shapes=[
                pltpu.VMEM((2, rows, width // 2), jnp.bfloat16),
                pltpu.VMEM((4, rows, feats), jnp.bfloat16),
            ],
        ),
        out_shape=[head, head, term, term],
        compiler_params=params(),
        cost_estimate=pl.CostEstimate(
            flops=8 * rows * width * feats + 16 * rows * rows * width,
            bytes_accessed=8 * width * feats + 16 * rows * triple,
            transcendentals=0,
        ),
        name="attend",
    )(at, kept, back, over, *stale, tables, gains, *columns)


def shards_four(
    latent,
    timestep,
    positions,
    modulation,
    qkv_weight,
    out_weight,
    query_gain,
    key_gain,
    stale_keys,
    stale_values,
):
    samples, rows, part_width = latent.shape
    size = query_gain.shape[0]
    f = lax.axis_index("fsdp")
    z = lax.axis_index("patch")
    y = lax.axis_index("rep")

    def to_f(v, d):
        return lax.ppermute(v, "fsdp", [(i, i ^ d) for i in range(4)])

    def to_y(v):
        return lax.ppermute(v, "rep", [(0, 1), (1, 0)])

    def to_z(v, d):
        return lax.ppermute(v, "patch", [(i, i ^ d) for i in range(4)])

    def after(v, *deps):
        return lax.optimization_barrier((v, *deps))[0]

    stale = jnp.stack([stale_keys, stale_values])
    s_x = to_f(stale, 2)
    own = [latent[s] for s in range(samples)]
    one, two, three = [], [], []
    for s in range(samples):
        start = own[s] if s == 0 else after(own[s], one[s - 1], two[s - 1])
        one.append(to_z(start, 1))
        two.append(to_z(start, 2))
        three.append(to_z(after(two[s], s_x), 1))

    picked = pick_rows(timestep, modulation)
    gate = picked[:, 2, :].astype(jnp.float32)[:, None, :]
    turn = picked[:, :2]
    turns = jnp.stack([turn] + [to_z(turn, d) for d in (1, 2, 3)])

    deep = out_weight.shape[0] // 2
    o_half = lax.dynamic_slice_in_dim(out_weight, y * deep, deep, 0)
    o_x = to_f(after(o_half, s_x), 2)
    o_xo = to_y(o_x)
    columns = (out_weight, to_f(out_weight, 1), o_x, o_xo, to_f(o_x, 1), to_f(o_xo, 1))
    stale_seen = (to_f(stale, 1), s_x, to_f(s_x, 1))

    quarter = size // 4
    freq = 10000.0 ** (-jnp.arange(quarter, dtype=jnp.float32) / quarter)
    row_angle = (positions // GRID_W).astype(jnp.float32)[:, None] * freq
    col_angle = (positions % GRID_W).astype(jnp.float32)[:, None] * freq
    row_sin, col_sin = jnp.sin(row_angle), jnp.sin(col_angle)
    row_cos, col_cos = jnp.cos(row_angle), jnp.cos(col_angle)
    tables = jnp.stack(
        [
            jnp.concatenate([row_cos, row_cos, col_cos, col_cos], axis=-1),
            jnp.concatenate([-row_sin, row_sin, -col_sin, col_sin], axis=-1),
        ]
    )
    gains = jnp.stack([query_gain, key_gain])
    key = f ^ z
    at = jnp.stack([key, y]).astype(jnp.int32)

    weight = qkv_weight.transpose(1, 0, 2)
    fence = o_x
    shared = []
    for s in range(samples):
        modded = run_norm(at, (own[s], one[s], two[s], three[s]), turns[:, s])
        over = to_f(after(modded[2], fence), 2)
        cross = to_f(after(modded[3], fence), 3)
        fence = over
        shared.append((modded[0], to_f(modded[1], 1), over, cross))
    keys, values, outs = [], [], []
    for s in range(samples):
        kept, sent = run_project(*shared[s], weight)
        back = to_f(sent, 1)
        part = (kept[1] + back[1]).astype(jnp.bfloat16)
        over = to_f(after(part, o_xo) if s == 0 else part, 2)
        new_keys, new_values, near, far = run_attend(
            s, at, kept, back, over, stale_seen, tables, gains, columns
        )
        keys.append(new_keys)
        values.append(new_values)
        come = to_z(far, 1)
        pair = near.astype(jnp.float32) + come.astype(jnp.float32)
        rest = to_z(pair[1].astype(jnp.bfloat16), 2)
        attended = pair[0] + rest.astype(jnp.float32)
        outs.append((own[s].astype(jnp.float32) + gate[s] * attended).astype(jnp.bfloat16))
    return (jnp.stack(outs), jnp.stack(keys), jnp.stack(values))


def solution(mesh):
    in_specs = (
        P("rep", "fsdp", "patch"),
        P("rep"),
        P(("rep", "fsdp")),
        P(None, None, "patch"),
        P("fsdp", None, "patch"),
        P("patch", "fsdp"),
        P(),
        P(),
        P("rep", "fsdp", "patch"),
        P("rep", "fsdp", "patch"),
    )
    out_specs = (P("rep", "fsdp", "patch"), P("rep", "fsdp", "patch"), P("rep", "fsdp", "patch"))
    four = (mesh.shape["rep"], mesh.shape["fsdp"], mesh.shape["patch"]) == (2, 4, 4)
    step = shards_four if four else shards_any
    return jax.shard_map(step, mesh=mesh, in_specs=in_specs, out_specs=out_specs, check_vma=False)
```

```python
import functools

import jax
import jax.numpy as jnp
from jax import lax
from jax.experimental import pallas as pl
from jax.experimental.pallas import tpu as pltpu
from jax.sharding import PartitionSpec as P

GRID_W = 62


EPS = 1e-06


def norm_heads(values, gain):
    return values * lax.rsqrt(jnp.mean(values * values, axis=-1, keepdims=True) + EPS) * gain


def rotate(values, places):
    quarter = values.shape[-1] // 4
    freq = 10000.0 ** (-jnp.arange(quarter, dtype=jnp.float32) / quarter)
    row_pos = (places // GRID_W).astype(jnp.float32)
    col_pos = (places % GRID_W).astype(jnp.float32)
    pieces = []
    for coords, lower in ((row_pos, 0), (col_pos, 2 * quarter)):
        angle = coords[:, None] * freq[None, :]
        cosine = jnp.cos(angle)[None, :, None, :]
        sine = jnp.sin(angle)[None, :, None, :]
        first = values[..., lower : lower + quarter]
        second = values[..., lower + quarter : lower + 2 * quarter]
        pieces.append(first * cosine - second * sine)
        pieces.append(second * cosine + first * sine)
    return jnp.concatenate(pieces, axis=-1)


def pick_rows(timestep, modulation):
    levels = modulation.shape[0]
    onehot = (timestep[:, None] == jnp.arange(levels, dtype=jnp.int32)[None, :]).astype(
        jnp.bfloat16
    )
    return jnp.einsum(
        "st,tcf->scf", onehot, modulation, preferred_element_type=jnp.float32
    ).astype(jnp.bfloat16)


def shards_any(
    latent,
    timestep,
    positions,
    modulation,
    qkv_weight,
    out_weight,
    query_gain,
    key_gain,
    stale_keys,
    stale_values,
):
    samples, rows, part_width = latent.shape
    head_size = query_gain.shape[0]
    local_width = qkv_weight.shape[2]
    heads = local_width // head_size
    mine = lax.axis_index("fsdp")
    factor = 1.0 / head_size**0.5
    picked = pick_rows(timestep, modulation)
    gate = picked[:, 2, :].astype(jnp.float32)[:, None, :]
    whole, mod_whole = (
        lax.all_gather(latent, "patch", axis=2, tiled=True),
        lax.all_gather(picked, "patch", axis=2, tiled=True),
    )
    values = whole.astype(jnp.float32)
    mean = jnp.mean(values, axis=-1, keepdims=True)
    centered = values - mean
    spread = jnp.mean(centered * centered, axis=-1, keepdims=True)
    shift = mod_whole[:, 0].astype(jnp.float32)[:, None, :]
    scale = mod_whole[:, 1].astype(jnp.float32)[:, None, :]
    modded = (centered * lax.rsqrt(spread + EPS) * (1.0 + scale) + shift).astype(jnp.bfloat16)
    projected = jnp.einsum(
        "std,dch->stch",
        modded,
        lax.all_gather(qkv_weight, "fsdp", axis=0, tiled=True),
        preferred_element_type=jnp.float32,
    )
    queries = rotate(
        norm_heads(projected[:, :, 0].reshape(samples, rows, heads, head_size), query_gain),
        positions,
    ).astype(jnp.bfloat16)
    fresh_keys = rotate(
        norm_heads(projected[:, :, 1].reshape(samples, rows, heads, head_size), key_gain), positions
    ).astype(jnp.bfloat16)
    fresh_flat = projected[:, :, 2].astype(jnp.bfloat16)
    fresh_values = fresh_flat.reshape(samples, rows, heads, head_size)
    scores = (
        jnp.einsum("sqhd,skhd->shqk", queries, fresh_keys, preferred_element_type=jnp.float32)
        * factor
    )
    top = jnp.max(scores, axis=-1)
    weights = jnp.exp(scores - top[..., None])
    total = jnp.sum(weights, axis=-1)
    summed = jnp.einsum(
        "shqk,skhd->shqd",
        weights.astype(jnp.bfloat16),
        fresh_values,
        preferred_element_type=jnp.float32,
    )
    own_low = mine * rows
    run_total = total
    run_sum = summed
    key_piece = lax.all_gather(stale_keys, "fsdp", axis=1, tiled=True).reshape(
        samples, -1, heads, head_size
    )
    value_piece = lax.all_gather(stale_values, "fsdp", axis=1, tiled=True).reshape(
        samples, -1, heads, head_size
    )
    count = key_piece.shape[1]
    piece_scores = (
        jnp.einsum("sqhd,skhd->shqk", queries, key_piece, preferred_element_type=jnp.float32)
        * factor
    )
    index = jnp.arange(count, dtype=jnp.int32)
    skipped = (index >= own_low) & (index < own_low + rows)
    piece_scores = jnp.where(skipped[None, None, None, :], -1e30, piece_scores)
    new_top = jnp.maximum(top, jnp.max(piece_scores, axis=-1))
    piece_weights = jnp.exp(piece_scores - new_top[..., None])
    fade = jnp.exp(top - new_top)
    run_total = run_total * fade + jnp.sum(piece_weights, axis=-1)
    run_sum = run_sum * fade[..., None] + jnp.einsum(
        "shqk,skhd->shqd",
        piece_weights.astype(jnp.bfloat16),
        value_piece,
        preferred_element_type=jnp.float32,
    )
    mixed = (
        (run_sum / run_total[..., None])
        .transpose(0, 2, 1, 3)
        .reshape(samples, rows, local_width)
        .astype(jnp.bfloat16)
    )
    terms = jnp.einsum(
        "sth,hn->stn",
        mixed,
        lax.all_gather(out_weight, "fsdp", axis=1, tiled=True),
        preferred_element_type=jnp.float32,
    )
    attended = lax.psum_scatter(
        terms.astype(jnp.bfloat16), "patch", scatter_dimension=2, tiled=True
    ).astype(jnp.float32)
    block_out = (latent.astype(jnp.float32) + gate * attended).astype(jnp.bfloat16)
    return (block_out, fresh_keys.reshape(samples, rows, local_width), fresh_flat)


def pack_kernel(timestep, latent, modulation, packed, gates):
    samples, feats = gates.shape
    rows = latent.shape[1]
    packed[:rows] = latent[0]
    level = lax.broadcasted_iota(jnp.int32, modulation.shape[1:], 0)
    picked = []
    for s in range(samples):
        here = level == timestep[s]
        for k in range(3):
            kept = jnp.where(here, modulation[k].astype(jnp.float32), 0.0)
            picked.append(jnp.sum(kept, axis=0, keepdims=True))
        gates[s : s + 1] = picked.pop()
    fill = jnp.zeros((packed.shape[0] - rows - 2 * samples, feats), jnp.float32)
    packed[rows:] = jnp.concatenate([*picked, fill], axis=0).astype(jnp.bfloat16)


def norm_kernel(s, key, *refs):
    blocks, turns, outs, held = refs[:4], refs[4:8], refs[8:12], refs[12]
    rows, feats = outs[0].shape
    mean = sum(
        jnp.sum(b[:rows].astype(jnp.float32), axis=-1, keepdims=True) for b in blocks
    ) / (4 * feats)
    spread = sum(
        jnp.sum(jnp.square(b[:rows].astype(jnp.float32) - mean), axis=-1, keepdims=True)
        for b in blocks
    ) / (4 * feats)
    rate = lax.rsqrt(spread + EPS)
    for r, (block, turn) in enumerate(zip(blocks, turns)):
        low = turn[rows:].astype(jnp.float32)
        shift = low[2 * s : 2 * s + 1]
        scale = low[2 * s + 1 : 2 * s + 2]
        centered = block[:rows].astype(jnp.float32) - mean
        held[r ^ key[0]] = (centered * rate * (1.0 + scale) + shift).astype(jnp.bfloat16)
    for j in range(4):
        outs[j][...] = held[j]


def project_kernel(first, second, weight, out, held):
    rows = first.shape[0]

    @pl.when(pl.program_id(0) == 0)
    def _():
        held[:rows] = first[...]
        held[rows:] = second[...]

    product = jnp.dot(held[...], weight[0], preferred_element_type=jnp.float32)
    out[0] = product[:rows]
    out[1] = product[rows:]


def attend_kernel(
    at, kept, back, over, k_pair, v_pair, k_x, v_x, k_d, v_d, tables, gains,
    o_own, o_pair, o_x, o_xa, o_xb, o_d, o_da, o_db,
    keys_out, values_out, near, far_one, far_three, mixed, held, columns, sems,
):
    rows, width = keys_out.shape
    size = gains.shape[1]
    half = mixed.shape[2]
    factor = 1.0 / size**0.5
    lane = lax.broadcasted_iota(jnp.int32, (rows, size), 1)
    low = (lane // (size // 4)) % 2 == 0
    rep = at[1]
    copies = []
    for j, refs in enumerate(((o_own,), (o_pair,), (o_x, o_xa, o_xb), (o_d, o_da, o_db))):
        start = 0
        for ref in refs:
            part = columns.at[j, start : start + ref.shape[0]]
            copy = pltpu.make_async_copy(ref, part, sems.at[len(copies)])
            copy.start()
            copies.append(copy)
            start += ref.shape[0]

    def summed(first):
        cols = slice(first, first + size)
        return kept[0, :, cols] + back[0, :, cols] + over[:, cols].astype(jnp.float32)

    def turned(values, gain):
        values = values * lax.rsqrt(jnp.mean(values * values, axis=-1, keepdims=True) + EPS) * gain
        other = jnp.where(
            low, pltpu.roll(values, size - size // 4, 1), pltpu.roll(values, size // 4, 1)
        )
        return (values * tables[0] + other * tables[1]).astype(jnp.bfloat16)

    for h in range(width // size):
        cols = slice(h * size, (h + 1) * size)
        query = turned(summed(h * size), gains[0:1])
        key = turned(summed(width + h * size), gains[1:2])
        value = summed(2 * width + h * size).astype(jnp.bfloat16)
        keys_out[:, cols] = key
        values_out[:, cols] = value
        keys = jnp.concatenate([key] + [s[0, :, cols] for s in (k_pair, k_x, k_d)], axis=0)
        seen = jnp.concatenate([value] + [s[0, :, cols] for s in (v_pair, v_x, v_d)], axis=0)
        scores = (
            lax.dot_general(
                query, keys, (((1,), (1,)), ((), ())), preferred_element_type=jnp.float32
            )
            * factor
        )
        weights = jnp.exp(scores - jnp.max(scores, axis=-1, keepdims=True))
        total = jnp.sum(weights, axis=-1, keepdims=True)
        product = jnp.dot(weights.astype(jnp.bfloat16), seen, preferred_element_type=jnp.float32)
        place = h * size // half
        start = h * size - place * half
        mixed[place, :, start : start + size] = (product / total).astype(jnp.bfloat16)

    for copy in copies:
        copy.wait()
    for j in range(4):
        one, two = (0, 1) if j < 2 else (rep, 1 - rep)
        term = jnp.dot(mixed[one], columns[j, :half], preferred_element_type=jnp.float32) + jnp.dot(
            mixed[two], columns[j, half:], preferred_element_type=jnp.float32
        )
        held[j ^ at[0]] = term.astype(jnp.bfloat16)
    near[0] = held[0]
    near[1] = held[2]
    far_one[...] = held[1]
    far_three[...] = held[3]


def params(mebibytes):
    return pltpu.CompilerParams(vmem_limit_bytes=mebibytes * 1024 * 1024)


def run_pack(timestep, latent, modulation):
    samples, rows, feats = latent.shape
    vmem = pl.BlockSpec(memory_space=pltpu.VMEM)
    return pl.pallas_call(
        pack_kernel,
        in_specs=[pl.BlockSpec(memory_space=pltpu.SMEM), vmem, vmem],
        out_specs=[vmem, vmem],
        out_shape=[
            jax.ShapeDtypeStruct((rows + 16, feats), jnp.bfloat16),
            jax.ShapeDtypeStruct((samples, feats), jnp.float32),
        ],
        compiler_params=params(16),
        name="pack",
    )(timestep, latent, modulation.transpose(1, 0, 2))


def run_norm(s, key, blocks, turns):
    rows = blocks[-1].shape[0] if s else blocks[-1].shape[0] - 16
    cols = blocks[0].shape[1]
    vmem = pl.BlockSpec(memory_space=pltpu.VMEM)
    shape = jax.ShapeDtypeStruct((rows, cols), jnp.bfloat16)
    return pl.pallas_call(
        functools.partial(norm_kernel, s),
        in_specs=[pl.BlockSpec(memory_space=pltpu.SMEM)] + [vmem] * 8,
        out_specs=[vmem] * 4,
        out_shape=[shape] * 4,
        scratch_shapes=[pltpu.VMEM((4, rows, cols), jnp.bfloat16)],
        compiler_params=params(16),
        cost_estimate=pl.CostEstimate(
            flops=60 * rows * cols, bytes_accessed=16 * rows * cols, transcendentals=0
        ),
        name="norm",
    )(key, *blocks, *turns)


def run_project(first, second, weight):
    rows, depth = first.shape
    wide = weight.shape[2]
    vmem = pl.BlockSpec((rows, depth), lambda i: (0, 0))
    return pl.pallas_call(
        project_kernel,
        grid=(3,),
        in_specs=[vmem] * 2 + [pl.BlockSpec((1, depth, wide), lambda i: (i, 0, 0))],
        out_specs=pl.BlockSpec((2, rows, wide), lambda i: (0, 0, i)),
        out_shape=jax.ShapeDtypeStruct((2, rows, 3 * wide), jnp.float32),
        scratch_shapes=[pltpu.VMEM((2 * rows, depth), jnp.bfloat16)],
        compiler_params=params(24),
        cost_estimate=pl.CostEstimate(
            flops=12 * rows * depth * wide,
            bytes_accessed=6 * depth * wide + 24 * rows * wide,
            transcendentals=0,
        ),
        name="project",
    )(first, second, weight)


def run_attend(s, at, kept, back, over, stale, tables, gains, columns):
    rows, triple = over.shape
    width = triple // 3
    feats = columns[0].shape[1]
    full = pl.BlockSpec(memory_space=pltpu.VMEM)
    first = pl.BlockSpec((1, rows, triple), lambda i, at: (0, 0, 0))
    seen = pl.BlockSpec((1, rows, width), lambda i, at: (s, 0, 0))
    head = jax.ShapeDtypeStruct((rows, width), jnp.bfloat16)
    term = jax.ShapeDtypeStruct((rows, feats), jnp.bfloat16)
    return pl.pallas_call(
        attend_kernel,
        grid_spec=pltpu.PrefetchScalarGridSpec(
            num_scalar_prefetch=1,
            grid=(1,),
            in_specs=[first, first, full]
            + [seen] * 6
            + [full] * 2
            + [pl.BlockSpec(memory_space=pl.ANY)] * 8,
            out_specs=[full] * 5,
            scratch_shapes=[
                pltpu.VMEM((2, rows, width // 2), jnp.bfloat16),
                pltpu.VMEM((4, rows, feats), jnp.bfloat16),
                pltpu.VMEM((4, width, feats), jnp.bfloat16),
                pltpu.SemaphoreType.DMA((8,)),
            ],
        ),
        out_shape=[head, head, jax.ShapeDtypeStruct((2, rows, feats), jnp.bfloat16), term, term],
        compiler_params=params(28),
        cost_estimate=pl.CostEstimate(
            flops=8 * rows * width * feats + 16 * rows * rows * width,
            bytes_accessed=8 * width * feats + 16 * rows * triple,
            transcendentals=0,
        ),
        name="attend",
    )(at, kept, back, over, *stale, tables, gains, *columns)


def shards_four(
    latent,
    timestep,
    positions,
    modulation,
    qkv_weight,
    out_weight,
    query_gain,
    key_gain,
    stale_keys,
    stale_values,
):
    samples, rows, part_width = latent.shape
    size = query_gain.shape[0]
    f = lax.axis_index("fsdp")
    z = lax.axis_index("patch")
    y = lax.axis_index("rep")

    def to_f(v, d):
        return lax.ppermute(v, "fsdp", [(i, i ^ d) for i in range(4)])

    def to_y(v):
        return lax.ppermute(v, "rep", [(0, 1), (1, 0)])

    def to_z(v, d):
        return lax.ppermute(v, "patch", [(i, i ^ d) for i in range(4)])

    def after(v, *deps):
        return lax.optimization_barrier((v, *deps))[0]

    packed, gate = run_pack(timestep, latent, modulation)
    own = [packed, latent[1]]
    two, one, three = [], [], []
    for s in range(samples):
        start = own[s] if s == 0 else after(own[s], one[-1], two[-1])
        two.append(to_z(start, 2))
        one.append(to_z(start, 1))
        three.append(to_z(two[s], 1))
    turns = (own[0], one[0], two[0], three[0])

    deep = out_weight.shape[0] // 2
    o_half = lax.dynamic_slice_in_dim(out_weight, y * deep, deep, 0)
    o_x = to_f(o_half, 2)
    k_x, v_x = to_f(after(stale_keys, o_x), 2), to_f(after(stale_values, o_x), 2)
    o_xa = to_y(o_x[: deep // 2])
    o_xb = to_y(after(o_x[deep // 2 :], o_xa))
    over_x = (o_x, o_xa, o_xb)
    columns = (out_weight, to_f(out_weight, 1), *over_x, *[to_f(v, 1) for v in over_x])
    stale_seen = (to_f(stale_keys, 1), to_f(stale_values, 1), k_x, v_x, to_f(k_x, 1), to_f(v_x, 1))

    quarter = size // 4
    freq = 10000.0 ** (-jnp.arange(quarter, dtype=jnp.float32) / quarter)
    row_angle = (positions // GRID_W).astype(jnp.float32)[:, None] * freq
    col_angle = (positions % GRID_W).astype(jnp.float32)[:, None] * freq
    row_sin, col_sin = jnp.sin(row_angle), jnp.sin(col_angle)
    row_cos, col_cos = jnp.cos(row_angle), jnp.cos(col_angle)
    tables = jnp.stack(
        [
            jnp.concatenate([row_cos, row_cos, col_cos, col_cos], axis=-1),
            jnp.concatenate([-row_sin, row_sin, -col_sin, col_sin], axis=-1),
        ]
    )
    gains = jnp.stack([query_gain, key_gain])
    key = f ^ z
    at = jnp.stack([key, y]).astype(jnp.int32)

    weight = qkv_weight.transpose(1, 0, 2)
    fence = (k_x, v_x)
    shared, normed = [], []
    for s in range(samples):
        modded = run_norm(s, at, (own[s], one[s], two[s], three[s]), turns)
        over = to_f(after(modded[2], *fence), 2)
        cross = to_f(after(modded[3], *fence), 3)
        fence = (over, cross)
        normed.append(modded[0])
        shared.append((modded[0], to_f(modded[1], 1), over, cross))
    halves, turned = [], []
    for s in range(samples):
        mine, pair, over, cross = shared[s]
        cross = after(cross, over, o_xa, *normed) if s == 0 else after(cross, over, o_xb, part)
        sent = run_project(pair, cross, weight)
        back = to_f(sent, 1)
        kept = run_project(mine, over, weight)
        part = (kept[1] + back[1]).astype(jnp.bfloat16)
        halves.append((kept, back))
        turned.append(to_f(after(part, *turned), 2))
    keys, values, outs = [], [], []
    for s in range(samples):
        kept, back = halves[s]
        new_keys, new_values, near, far_one, far_three = run_attend(
            s, at, kept, back, turned[s], stale_seen, tables, gains, columns
        )
        keys.append(new_keys)
        values.append(new_values)
        come = to_z(far_three, 1)
        rest = to_z((near[1].astype(jnp.float32) + come.astype(jnp.float32)).astype(jnp.bfloat16), 2)
        come = to_z(far_one, 1)
        attended = (near[0].astype(jnp.float32) + come.astype(jnp.float32)) + rest.astype(jnp.float32)
        outs.append((latent[s].astype(jnp.float32) + gate[s] * attended).astype(jnp.bfloat16))
    return (jnp.stack(outs), jnp.stack(keys), jnp.stack(values))


def solution(mesh):
    in_specs = (
        P("rep", "fsdp", "patch"),
        P("rep"),
        P(("rep", "fsdp")),
        P(None, None, "patch"),
        P("fsdp", None, "patch"),
        P("patch", "fsdp"),
        P(),
        P(),
        P("rep", "fsdp", "patch"),
        P("rep", "fsdp", "patch"),
    )
    out_specs = (P("rep", "fsdp", "patch"), P("rep", "fsdp", "patch"), P("rep", "fsdp", "patch"))
    four = (mesh.shape["rep"], mesh.shape["fsdp"], mesh.shape["patch"]) == (2, 4, 4)
    step = shards_four if four else shards_any
    return jax.shard_map(step, mesh=mesh, in_specs=in_specs, out_specs=out_specs, check_vma=False)
```

```python
import functools

import jax
import jax.numpy as jnp
from jax import lax
from jax.experimental import pallas as pl
from jax.experimental.pallas import tpu as pltpu
from jax.sharding import PartitionSpec as P

GRID_W = 62


EPS = 1e-06


def norm_heads(values, gain):
    return values * lax.rsqrt(jnp.mean(values * values, axis=-1, keepdims=True) + EPS) * gain


def rotate(values, places):
    quarter = values.shape[-1] // 4
    freq = 10000.0 ** (-jnp.arange(quarter, dtype=jnp.float32) / quarter)
    row_pos = (places // GRID_W).astype(jnp.float32)
    col_pos = (places % GRID_W).astype(jnp.float32)
    pieces = []
    for coords, lower in ((row_pos, 0), (col_pos, 2 * quarter)):
        angle = coords[:, None] * freq[None, :]
        cosine = jnp.cos(angle)[None, :, None, :]
        sine = jnp.sin(angle)[None, :, None, :]
        first = values[..., lower : lower + quarter]
        second = values[..., lower + quarter : lower + 2 * quarter]
        pieces.append(first * cosine - second * sine)
        pieces.append(second * cosine + first * sine)
    return jnp.concatenate(pieces, axis=-1)


def pick_rows(timestep, modulation):
    levels = modulation.shape[0]
    onehot = (timestep[:, None] == jnp.arange(levels, dtype=jnp.int32)[None, :]).astype(
        jnp.bfloat16
    )
    return jnp.einsum(
        "st,tcf->scf", onehot, modulation, preferred_element_type=jnp.float32
    ).astype(jnp.bfloat16)


def shards_any(
    latent,
    timestep,
    positions,
    modulation,
    qkv_weight,
    out_weight,
    query_gain,
    key_gain,
    stale_keys,
    stale_values,
):
    samples, rows, part_width = latent.shape
    head_size = query_gain.shape[0]
    local_width = qkv_weight.shape[2]
    heads = local_width // head_size
    mine = lax.axis_index("fsdp")
    factor = 1.0 / head_size**0.5
    picked = pick_rows(timestep, modulation)
    gate = picked[:, 2, :].astype(jnp.float32)[:, None, :]
    whole, mod_whole = (
        lax.all_gather(latent, "patch", axis=2, tiled=True),
        lax.all_gather(picked, "patch", axis=2, tiled=True),
    )
    values = whole.astype(jnp.float32)
    mean = jnp.mean(values, axis=-1, keepdims=True)
    centered = values - mean
    spread = jnp.mean(centered * centered, axis=-1, keepdims=True)
    shift = mod_whole[:, 0].astype(jnp.float32)[:, None, :]
    scale = mod_whole[:, 1].astype(jnp.float32)[:, None, :]
    modded = (centered * lax.rsqrt(spread + EPS) * (1.0 + scale) + shift).astype(jnp.bfloat16)
    projected = jnp.einsum(
        "std,dch->stch",
        modded,
        lax.all_gather(qkv_weight, "fsdp", axis=0, tiled=True),
        preferred_element_type=jnp.float32,
    )
    queries = rotate(
        norm_heads(projected[:, :, 0].reshape(samples, rows, heads, head_size), query_gain),
        positions,
    ).astype(jnp.bfloat16)
    fresh_keys = rotate(
        norm_heads(projected[:, :, 1].reshape(samples, rows, heads, head_size), key_gain), positions
    ).astype(jnp.bfloat16)
    fresh_flat = projected[:, :, 2].astype(jnp.bfloat16)
    fresh_values = fresh_flat.reshape(samples, rows, heads, head_size)
    scores = (
        jnp.einsum("sqhd,skhd->shqk", queries, fresh_keys, preferred_element_type=jnp.float32)
        * factor
    )
    top = jnp.max(scores, axis=-1)
    weights = jnp.exp(scores - top[..., None])
    total = jnp.sum(weights, axis=-1)
    summed = jnp.einsum(
        "shqk,skhd->shqd",
        weights.astype(jnp.bfloat16),
        fresh_values,
        preferred_element_type=jnp.float32,
    )
    own_low = mine * rows
    run_total = total
    run_sum = summed
    key_piece = lax.all_gather(stale_keys, "fsdp", axis=1, tiled=True).reshape(
        samples, -1, heads, head_size
    )
    value_piece = lax.all_gather(stale_values, "fsdp", axis=1, tiled=True).reshape(
        samples, -1, heads, head_size
    )
    count = key_piece.shape[1]
    piece_scores = (
        jnp.einsum("sqhd,skhd->shqk", queries, key_piece, preferred_element_type=jnp.float32)
        * factor
    )
    index = jnp.arange(count, dtype=jnp.int32)
    skipped = (index >= own_low) & (index < own_low + rows)
    piece_scores = jnp.where(skipped[None, None, None, :], -1e30, piece_scores)
    new_top = jnp.maximum(top, jnp.max(piece_scores, axis=-1))
    piece_weights = jnp.exp(piece_scores - new_top[..., None])
    fade = jnp.exp(top - new_top)
    run_total = run_total * fade + jnp.sum(piece_weights, axis=-1)
    run_sum = run_sum * fade[..., None] + jnp.einsum(
        "shqk,skhd->shqd",
        piece_weights.astype(jnp.bfloat16),
        value_piece,
        preferred_element_type=jnp.float32,
    )
    mixed = (
        (run_sum / run_total[..., None])
        .transpose(0, 2, 1, 3)
        .reshape(samples, rows, local_width)
        .astype(jnp.bfloat16)
    )
    terms = jnp.einsum(
        "sth,hn->stn",
        mixed,
        lax.all_gather(out_weight, "fsdp", axis=1, tiled=True),
        preferred_element_type=jnp.float32,
    )
    attended = lax.psum_scatter(
        terms.astype(jnp.bfloat16), "patch", scatter_dimension=2, tiled=True
    ).astype(jnp.float32)
    block_out = (latent.astype(jnp.float32) + gate * attended).astype(jnp.bfloat16)
    return (block_out, fresh_keys.reshape(samples, rows, local_width), fresh_flat)


def pack_kernel(timestep, latent, modulation, packed, gates):
    samples, feats = gates.shape
    rows = latent.shape[1]
    packed[:rows] = latent[0]
    level = lax.broadcasted_iota(jnp.int32, modulation.shape[1:], 0)
    picked = []
    for s in range(samples):
        here = level == timestep[s]
        for k in range(3):
            kept = jnp.where(here, modulation[k].astype(jnp.float32), 0.0)
            picked.append(jnp.sum(kept, axis=0, keepdims=True))
        gates[s : s + 1] = picked.pop()
    fill = jnp.zeros((packed.shape[0] - rows - 2 * samples, feats), jnp.float32)
    packed[rows:] = jnp.concatenate([*picked, fill], axis=0).astype(jnp.bfloat16)


def norm_kernel(s, key, *refs):
    blocks, turns, (mine, pair, far, held) = refs[:4], refs[4:8], refs[8:]
    rows, feats = mine.shape

    def block(r):
        return blocks[r][:rows].astype(jnp.float32)

    mean = sum(jnp.sum(block(r), axis=-1, keepdims=True) for r in range(4)) / (4 * feats)
    spread = sum(
        jnp.sum(jnp.square(block(r) - mean), axis=-1, keepdims=True) for r in range(4)
    ) / (4 * feats)
    rate = lax.rsqrt(spread + EPS)
    for r, turn in enumerate(turns):
        low = turn[rows : rows + 16].astype(jnp.float32)
        shift = low[2 * s : 2 * s + 1]
        scale = low[2 * s + 1 : 2 * s + 2]
        held[r ^ key[0]] = ((block(r) - mean) * rate * (1.0 + scale) + shift).astype(jnp.bfloat16)
    mine[...] = held[0]
    pair[...] = held[1]
    far[:rows] = held[2]
    far[rows:] = held[3]


def project_kernel(first, second, weight, out, held):
    rows = first.shape[0]

    @pl.when(pl.program_id(0) == 0)
    def _():
        held[:rows] = first[...]
        held[rows:] = second[...]

    product = jnp.dot(held[...], weight[0], preferred_element_type=jnp.float32)
    out[0] = product[:rows]
    out[1] = product[rows:]


def attend_kernel(
    at, kept, back, over, k_pair, v_pair, k_x, v_x, k_d, v_d, tables, gains,
    o_own, o_pair, o_x, o_y, o_d, o_dy,
    keys_out, values_out, near, far_one, far_three, mixed, held, columns, sems,
):
    rows, width = keys_out.shape
    size = gains.shape[1]
    half = mixed.shape[2]
    factor = 1.0 / size**0.5
    lane = lax.broadcasted_iota(jnp.int32, (rows, size), 1)
    low = (lane // (size // 4)) % 2 == 0
    rep = at[1]
    moves = [(o_own, columns.at[0]), (o_pair, columns.at[1])]
    for j, low_half, high_half in ((2, o_x, o_y), (3, o_d, o_dy)):
        for ref, first in ((low_half, 0), (high_half, half)):
            start = ref.shape[0] - 2 * half
            for k in range(2):
                part = columns.at[j, first : first + half, k * width : (k + 1) * width]
                moves.append((ref.at[start + k * half : start + (k + 1) * half], part))
    copies = [
        pltpu.make_async_copy(ref, part, sems.at[n]) for n, (ref, part) in enumerate(moves)
    ]
    for copy in copies:
        copy.start()

    def summed(first):
        cols = slice(first, first + size)
        return kept[0, :, cols] + back[0, :, cols] + over[:, cols].astype(jnp.float32)

    def turned(values, gain):
        values = values * lax.rsqrt(jnp.mean(values * values, axis=-1, keepdims=True) + EPS) * gain
        other = jnp.where(
            low, pltpu.roll(values, size - size // 4, 1), pltpu.roll(values, size // 4, 1)
        )
        return (values * tables[0] + other * tables[1]).astype(jnp.bfloat16)

    for h in range(width // size):
        cols = slice(h * size, (h + 1) * size)
        query = turned(summed(h * size), gains[0:1])
        key = turned(summed(width + h * size), gains[1:2])
        value = summed(2 * width + h * size).astype(jnp.bfloat16)
        keys_out[:, cols] = key
        values_out[:, cols] = value
        keys = jnp.concatenate([key] + [s[:, cols] for s in (k_pair, k_x, k_d)], axis=0)
        seen = jnp.concatenate([value] + [s[:, cols] for s in (v_pair, v_x, v_d)], axis=0)
        scores = (
            lax.dot_general(
                query, keys, (((1,), (1,)), ((), ())), preferred_element_type=jnp.float32
            )
            * factor
        )
        weights = jnp.exp(scores - jnp.max(scores, axis=-1, keepdims=True))
        total = jnp.sum(weights, axis=-1, keepdims=True)
        product = jnp.dot(weights.astype(jnp.bfloat16), seen, preferred_element_type=jnp.float32)
        place = h * size // half
        start = h * size - place * half
        mixed[place, :, start : start + size] = (product / total).astype(jnp.bfloat16)

    for copy in copies:
        copy.wait()
    for j in range(4):
        one, two = (0, 1) if j < 2 else (rep, 1 - rep)
        term = jnp.dot(mixed[one], columns[j, :half], preferred_element_type=jnp.float32) + jnp.dot(
            mixed[two], columns[j, half:], preferred_element_type=jnp.float32
        )
        held[j ^ at[0]] = term.astype(jnp.bfloat16)
    near[0] = held[0]
    near[1] = held[2]
    far_one[...] = held[1]
    far_three[...] = held[3]


TIES = {'kept1': ('cross_far',),
 'last1': ('rest0',),
 'late': ('two0',),
 'sent0': ('three1', 'o_pair', 's_pair'),
 'sent0_last': (),
 'sent1_last': (),
 'use1': ('kept0',)}
WORK = {'attend0': 6,
 'attend1': 9,
 'kept0': 9,
 'kept1': 11,
 'norm0': 8,
 'norm1': 9,
 'second': 10,
 'sent0': 9,
 'sent1': 9}


def cost(name):
    return pl.CostEstimate(flops=10 ** WORK[name], bytes_accessed=10**6, transcendentals=0)


def params(mebibytes):
    return pltpu.CompilerParams(vmem_limit_bytes=mebibytes * 1024 * 1024)


def run_pack(timestep, latent, modulation):
    samples, rows, feats = latent.shape
    vmem = pl.BlockSpec(memory_space=pltpu.VMEM)
    return pl.pallas_call(
        pack_kernel,
        in_specs=[pl.BlockSpec(memory_space=pltpu.SMEM), vmem, vmem],
        out_specs=[vmem, vmem],
        out_shape=[
            jax.ShapeDtypeStruct((rows + 16, feats), jnp.bfloat16),
            jax.ShapeDtypeStruct((samples, feats), jnp.float32),
        ],
        compiler_params=params(16),
        name="pack",
    )(timestep, latent, modulation.transpose(1, 0, 2))


def second_kernel(latent, out):
    out[...] = latent[0]


def run_second(latent):
    _, rows, feats = latent.shape
    return pl.pallas_call(
        second_kernel,
        grid=(1,),
        in_specs=[pl.BlockSpec((1, rows, feats), lambda i: (1, 0, 0))],
        out_specs=pl.BlockSpec((rows, feats), lambda i: (0, 0)),
        out_shape=jax.ShapeDtypeStruct((rows, feats), jnp.bfloat16),
        compiler_params=params(16),
        cost_estimate=cost("second"),
        name="second",
    )(latent)


def run_norm(s, key, rows, blocks, turns):
    cols = blocks[0].shape[1]
    vmem = pl.BlockSpec(memory_space=pltpu.VMEM)
    shape = jax.ShapeDtypeStruct((rows, cols), jnp.bfloat16)
    return pl.pallas_call(
        functools.partial(norm_kernel, s),
        in_specs=[pl.BlockSpec(memory_space=pltpu.SMEM)] + [vmem] * 8,
        out_specs=[vmem] * 3,
        out_shape=[shape, shape, jax.ShapeDtypeStruct((2 * rows, cols), jnp.bfloat16)],
        scratch_shapes=[pltpu.VMEM((4, rows, cols), jnp.bfloat16)],
        compiler_params=params(16),
        cost_estimate=cost(f"norm{s}"),
        name="norm",
    )(key, *blocks, *turns)


def run_project(name, first, second, weight):
    rows, depth = first.shape
    wide = weight.shape[2]
    vmem = pl.BlockSpec((rows, depth), lambda i: (0, 0))
    return pl.pallas_call(
        project_kernel,
        grid=(3,),
        in_specs=[vmem] * 2 + [pl.BlockSpec((1, depth, wide), lambda i: (i, 0, 0))],
        out_specs=pl.BlockSpec((2, rows, wide), lambda i: (0, 0, i)),
        out_shape=jax.ShapeDtypeStruct((2, rows, 3 * wide), jnp.float32),
        scratch_shapes=[pltpu.VMEM((2 * rows, depth), jnp.bfloat16)],
        compiler_params=params(24),
        cost_estimate=cost(name),
        name="project",
    )(first, second, weight)


def run_attend(s, at, kept, back, over, stale, tables, gains, columns):
    rows, triple = over.shape
    width = triple // 3
    feats = columns[0].shape[1]
    full = pl.BlockSpec(memory_space=pltpu.VMEM)
    first = pl.BlockSpec((1, rows, triple), lambda i, at: (0, 0, 0))
    samples = 2
    seen = [
        pl.BlockSpec((rows, width), lambda i, at: (s, 0)),
        pl.BlockSpec((rows, width), lambda i, at: (samples + s, 0)),
    ]
    head = jax.ShapeDtypeStruct((rows, width), jnp.bfloat16)
    term = jax.ShapeDtypeStruct((rows, feats), jnp.bfloat16)
    return pl.pallas_call(
        attend_kernel,
        grid_spec=pltpu.PrefetchScalarGridSpec(
            num_scalar_prefetch=1,
            grid=(1,),
            in_specs=[first, first, full]
            + seen * 3
            + [full] * 2
            + [pl.BlockSpec(memory_space=pl.ANY)] * 6,
            out_specs=[full] * 5,
            scratch_shapes=[
                pltpu.VMEM((2, rows, width // 2), jnp.bfloat16),
                pltpu.VMEM((4, rows, feats), jnp.bfloat16),
                pltpu.VMEM((4, width, feats), jnp.bfloat16),
                pltpu.SemaphoreType.DMA((10,)),
            ],
        ),
        out_shape=[head, head, jax.ShapeDtypeStruct((2, rows, feats), jnp.bfloat16), term, term],
        compiler_params=params(28),
        cost_estimate=cost(f"attend{s}"),
        name="attend",
    )(at, kept, back, over, *[v for v in stale for _ in range(2)], tables, gains, *columns)


def shards_four(
    latent,
    timestep,
    positions,
    modulation,
    qkv_weight,
    out_weight,
    query_gain,
    key_gain,
    stale_keys,
    stale_values,
):
    samples, rows, part_width = latent.shape
    size = query_gain.shape[0]
    f = lax.axis_index("fsdp")
    z = lax.axis_index("patch")
    y = lax.axis_index("rep")

    def to_f(v, d):
        return lax.ppermute(v, "fsdp", [(i, i ^ d) for i in range(4)])

    def to_y(v):
        return lax.ppermute(v, "rep", [(0, 1), (1, 0)])

    def to_z(v, d):
        return lax.ppermute(v, "patch", [(i, i ^ d) for i in range(4)])

    def after(v, *deps):
        return lax.optimization_barrier((v, *deps))[0]

    made = {}

    def make(name, value):
        made[name] = value
        return value

    def tie(name, value):
        deps = [made[dep] for dep in TIES.get(name, ())]
        return after(value, *deps) if deps else value

    quarter = size // 4
    freq = 10000.0 ** (-jnp.arange(quarter, dtype=jnp.float32) / quarter)
    row_angle = (positions // GRID_W).astype(jnp.float32)[:, None] * freq
    col_angle = (positions % GRID_W).astype(jnp.float32)[:, None] * freq
    row_sin, col_sin = jnp.sin(row_angle), jnp.sin(col_angle)
    row_cos, col_cos = jnp.cos(row_angle), jnp.cos(col_angle)
    tables = jnp.stack(
        [
            jnp.concatenate([row_cos, row_cos, col_cos, col_cos], axis=-1),
            jnp.concatenate([-row_sin, row_sin, -col_sin, col_sin], axis=-1),
        ]
    )
    gains = jnp.stack([query_gain, key_gain])
    key = f ^ z
    at = jnp.stack([key, y]).astype(jnp.int32)

    weight = qkv_weight.transpose(1, 0, 2)
    packed, gate = run_pack(timestep, latent, modulation)
    make("packed", packed)
    two, one, three = [make("two0", to_z(packed, 2))], [make("one0", to_z(packed, 1))], []
    three.append(make("three0", to_z(two[0], 1)))
    deep = out_weight.shape[0] // 2
    width = stale_keys.shape[2]
    o_half = lax.dynamic_slice_in_dim(out_weight, y * deep, deep, 0)
    stale = [v.reshape(samples * rows, width) for v in (stale_keys, stale_values)]
    cut = len(stale) * samples * rows
    far = jnp.concatenate([*stale, o_half[:, :width], o_half[:, width:]])
    far = make("far", to_f(tie("far", far), 2))
    late = run_second(tie("late", latent))
    two.append(make("two1", to_z(late, 2)))
    one.append(make("one1", to_z(tie("one1", late), 1)))
    three.append(make("three1", to_z(two[1], 1)))
    turns = (packed, one[0], two[0], three[0])
    blocks = (turns, (late, one[1], two[1], three[1]))

    shared = []
    for s in range(samples):
        last = tie(f"norm{s}", blocks[s][3])
        mine, pair, away = run_norm(s, at, rows, (*blocks[s][:3], last), turns)
        make(f"mine{s}", mine)
        away = make(f"away{s}", to_f(tie(f"away{s}", away), 2))
        pair = make(f"pair{s}", to_f(tie(f"pair{s}", pair), 1))
        shared.append((mine, pair, away))
    o_y = make("o_y", to_y(tie("o_y", far[cut:])))
    o_pair = make("o_pair", to_f(tie("o_pair", out_weight), 1))
    s_pair = make("s_pair", to_f(tie("s_pair", jnp.concatenate(stale)), 1))
    cross_far = make("cross_far", to_f(tie("cross_far", far), 1))
    halves, turned = [], []
    for s in range(samples):
        mine, pair, away = shared[s]
        away = tie(f"use{s}", away)
        over, cross = away[:rows], make(f"cross{s}", to_f(away[rows:], 1))
        if s == 1:
            cross_y = make("cross_y", to_f(tie("cross_y", o_y), 1))
        if f"sent{s}_last" in TIES:
            kept = make(f"kept{s}", run_project(f"kept{s}", tie(f"kept{s}", mine), over, weight))
            sent = run_project(f"sent{s}", pair, tie(f"sent{s}", cross), weight)
        else:
            sent = run_project(f"sent{s}", pair, tie(f"sent{s}", cross), weight)
            kept = make(f"kept{s}", run_project(f"kept{s}", tie(f"kept{s}", mine), over, weight))
        back = make(f"back{s}", to_f(sent, 1))
        part = make(f"part{s}", (kept[1] + back[1]).astype(jnp.bfloat16))
        halves.append((kept, back))
        turned.append(make(f"turned{s}", to_f(tie(f"turned{s}", part), 2)))
    columns = (out_weight, o_pair, far, o_y, cross_far, cross_y)
    stale_seen = (s_pair, far, cross_far)
    keys, values, outs = [], [], []
    for s in range(samples):
        kept, back = halves[s]
        new_keys, new_values, near, far_one, far_three = run_attend(
            s, at, kept, back, tie(f"attend{s}", turned[s]), stale_seen, tables, gains, columns
        )
        keys.append(new_keys)
        values.append(new_values)
        come = make(f"come{s}", to_z(far_three, 1))
        rest = near[1].astype(jnp.float32) + come.astype(jnp.float32)
        rest = make(f"rest{s}", to_z(rest.astype(jnp.bfloat16), 2))
        last = make(f"last{s}", to_z(tie(f"last{s}", far_one), 1))
        attended = (near[0].astype(jnp.float32) + last.astype(jnp.float32)) + rest.astype(jnp.float32)
        outs.append((latent[s].astype(jnp.float32) + gate[s] * attended).astype(jnp.bfloat16))
    return (jnp.stack(outs), jnp.stack(keys), jnp.stack(values))


def solution(mesh):
    in_specs = (
        P("rep", "fsdp", "patch"),
        P("rep"),
        P(("rep", "fsdp")),
        P(None, None, "patch"),
        P("fsdp", None, "patch"),
        P("patch", "fsdp"),
        P(),
        P(),
        P("rep", "fsdp", "patch"),
        P("rep", "fsdp", "patch"),
    )
    out_specs = (P("rep", "fsdp", "patch"), P("rep", "fsdp", "patch"), P("rep", "fsdp", "patch"))
    four = (mesh.shape["rep"], mesh.shape["fsdp"], mesh.shape["patch"]) == (2, 4, 4)
    step = shards_four if four else shards_any
    return jax.shard_map(step, mesh=mesh, in_specs=in_specs, out_specs=out_specs, check_vma=False)
```

```python
import functools

import jax
import jax.numpy as jnp
from jax import lax
from jax.experimental import pallas as pl
from jax.experimental.pallas import tpu as pltpu
from jax.sharding import PartitionSpec as P

GRID_W = 62


EPS = 1e-06


def norm_heads(values, gain):
    return values * lax.rsqrt(jnp.mean(values * values, axis=-1, keepdims=True) + EPS) * gain


def rotate(values, places):
    quarter = values.shape[-1] // 4
    freq = 10000.0 ** (-jnp.arange(quarter, dtype=jnp.float32) / quarter)
    row_pos = (places // GRID_W).astype(jnp.float32)
    col_pos = (places % GRID_W).astype(jnp.float32)
    pieces = []
    for coords, lower in ((row_pos, 0), (col_pos, 2 * quarter)):
        angle = coords[:, None] * freq[None, :]
        cosine = jnp.cos(angle)[None, :, None, :]
        sine = jnp.sin(angle)[None, :, None, :]
        first = values[..., lower : lower + quarter]
        second = values[..., lower + quarter : lower + 2 * quarter]
        pieces.append(first * cosine - second * sine)
        pieces.append(second * cosine + first * sine)
    return jnp.concatenate(pieces, axis=-1)


def pick_rows(timestep, modulation):
    levels = modulation.shape[0]
    onehot = (timestep[:, None] == jnp.arange(levels, dtype=jnp.int32)[None, :]).astype(
        jnp.bfloat16
    )
    return jnp.einsum(
        "st,tcf->scf", onehot, modulation, preferred_element_type=jnp.float32
    ).astype(jnp.bfloat16)


def shards_any(
    latent,
    timestep,
    positions,
    modulation,
    qkv_weight,
    out_weight,
    query_gain,
    key_gain,
    stale_keys,
    stale_values,
):
    samples, rows, part_width = latent.shape
    head_size = query_gain.shape[0]
    local_width = qkv_weight.shape[2]
    heads = local_width // head_size
    mine = lax.axis_index("fsdp")
    factor = 1.0 / head_size**0.5
    picked = pick_rows(timestep, modulation)
    gate = picked[:, 2, :].astype(jnp.float32)[:, None, :]
    whole, mod_whole = (
        lax.all_gather(latent, "patch", axis=2, tiled=True),
        lax.all_gather(picked, "patch", axis=2, tiled=True),
    )
    values = whole.astype(jnp.float32)
    mean = jnp.mean(values, axis=-1, keepdims=True)
    centered = values - mean
    spread = jnp.mean(centered * centered, axis=-1, keepdims=True)
    shift = mod_whole[:, 0].astype(jnp.float32)[:, None, :]
    scale = mod_whole[:, 1].astype(jnp.float32)[:, None, :]
    modded = (centered * lax.rsqrt(spread + EPS) * (1.0 + scale) + shift).astype(jnp.bfloat16)
    projected = jnp.einsum(
        "std,dch->stch",
        modded,
        lax.all_gather(qkv_weight, "fsdp", axis=0, tiled=True),
        preferred_element_type=jnp.float32,
    )
    queries = rotate(
        norm_heads(projected[:, :, 0].reshape(samples, rows, heads, head_size), query_gain),
        positions,
    ).astype(jnp.bfloat16)
    fresh_keys = rotate(
        norm_heads(projected[:, :, 1].reshape(samples, rows, heads, head_size), key_gain), positions
    ).astype(jnp.bfloat16)
    fresh_flat = projected[:, :, 2].astype(jnp.bfloat16)
    fresh_values = fresh_flat.reshape(samples, rows, heads, head_size)
    scores = (
        jnp.einsum("sqhd,skhd->shqk", queries, fresh_keys, preferred_element_type=jnp.float32)
        * factor
    )
    top = jnp.max(scores, axis=-1)
    weights = jnp.exp(scores - top[..., None])
    total = jnp.sum(weights, axis=-1)
    summed = jnp.einsum(
        "shqk,skhd->shqd",
        weights.astype(jnp.bfloat16),
        fresh_values,
        preferred_element_type=jnp.float32,
    )
    own_low = mine * rows
    run_total = total
    run_sum = summed
    key_piece = lax.all_gather(stale_keys, "fsdp", axis=1, tiled=True).reshape(
        samples, -1, heads, head_size
    )
    value_piece = lax.all_gather(stale_values, "fsdp", axis=1, tiled=True).reshape(
        samples, -1, heads, head_size
    )
    count = key_piece.shape[1]
    piece_scores = (
        jnp.einsum("sqhd,skhd->shqk", queries, key_piece, preferred_element_type=jnp.float32)
        * factor
    )
    index = jnp.arange(count, dtype=jnp.int32)
    skipped = (index >= own_low) & (index < own_low + rows)
    piece_scores = jnp.where(skipped[None, None, None, :], -1e30, piece_scores)
    new_top = jnp.maximum(top, jnp.max(piece_scores, axis=-1))
    piece_weights = jnp.exp(piece_scores - new_top[..., None])
    fade = jnp.exp(top - new_top)
    run_total = run_total * fade + jnp.sum(piece_weights, axis=-1)
    run_sum = run_sum * fade[..., None] + jnp.einsum(
        "shqk,skhd->shqd",
        piece_weights.astype(jnp.bfloat16),
        value_piece,
        preferred_element_type=jnp.float32,
    )
    mixed = (
        (run_sum / run_total[..., None])
        .transpose(0, 2, 1, 3)
        .reshape(samples, rows, local_width)
        .astype(jnp.bfloat16)
    )
    terms = jnp.einsum(
        "sth,hn->stn",
        mixed,
        lax.all_gather(out_weight, "fsdp", axis=1, tiled=True),
        preferred_element_type=jnp.float32,
    )
    attended = lax.psum_scatter(
        terms.astype(jnp.bfloat16), "patch", scatter_dimension=2, tiled=True
    ).astype(jnp.float32)
    block_out = (latent.astype(jnp.float32) + gate * attended).astype(jnp.bfloat16)
    return (block_out, fresh_keys.reshape(samples, rows, local_width), fresh_flat)


def pack_kernel(timestep, latent, modulation, packed, gates):
    samples, feats = gates.shape
    rows = latent.shape[1]
    packed[:rows] = latent[0]
    level = lax.broadcasted_iota(jnp.int32, modulation.shape[1:], 0)
    picked = []
    for s in range(samples):
        here = level == timestep[s]
        for k in range(3):
            kept = jnp.where(here, modulation[k].astype(jnp.float32), 0.0)
            picked.append(jnp.sum(kept, axis=0, keepdims=True))
        gates[s : s + 1] = picked.pop()
    fill = jnp.zeros((packed.shape[0] - rows - 2 * samples, feats), jnp.float32)
    packed[rows:] = jnp.concatenate([*picked, fill], axis=0).astype(jnp.bfloat16)


def norm_kernel(s, key, *refs):
    blocks, turns, (mine, pair, far, held) = refs[:4], refs[4:8], refs[8:]
    rows, feats = mine.shape

    def block(r):
        return blocks[r][:rows].astype(jnp.float32)

    mean = sum(jnp.sum(block(r), axis=-1, keepdims=True) for r in range(4)) / (4 * feats)
    spread = sum(
        jnp.sum(jnp.square(block(r) - mean), axis=-1, keepdims=True) for r in range(4)
    ) / (4 * feats)
    rate = lax.rsqrt(spread + EPS)
    for r, turn in enumerate(turns):
        low = turn[rows : rows + 16].astype(jnp.float32)
        shift = low[2 * s : 2 * s + 1]
        scale = low[2 * s + 1 : 2 * s + 2]
        held[r ^ key[0]] = ((block(r) - mean) * rate * (1.0 + scale) + shift).astype(jnp.bfloat16)
    mine[...] = held[0]
    pair[...] = held[1]
    far[:rows] = held[2]
    far[rows:] = held[3]


def project_kernel(first, second, weight, out, held):
    rows = first.shape[0]

    @pl.when(pl.program_id(0) == 0)
    def _():
        held[:rows] = first[...]
        held[rows:] = second[...]

    product = jnp.dot(held[...], weight[0], preferred_element_type=jnp.float32)
    out[0] = product[:rows]
    out[1] = product[rows:]


def merge_kernel(kept, back, out):
    out[...] = (kept[0] + back[0]).astype(jnp.bfloat16)


def attend_kernel(
    at, kept, back, over, k_pair, v_pair, k_x, v_x, k_d, v_d, tables, gains,
    o_own, o_pair, o_x, o_y, o_d, o_dy,
    keys_out, values_out, near, far_one, far_three, mixed, held, columns, sems,
):
    rows, width = keys_out.shape
    size = gains.shape[1]
    half = mixed.shape[2]
    factor = 1.0 / size**0.5
    lane = lax.broadcasted_iota(jnp.int32, (rows, size), 1)
    low = (lane // (size // 4)) % 2 == 0
    rep = at[1]
    moves = [(o_own, columns.at[0]), (o_pair, columns.at[1])]
    for j, low_half, high_half in ((2, o_x, o_y), (3, o_d, o_dy)):
        for ref, first in ((low_half, 0), (high_half, half)):
            start = ref.shape[0] - 2 * half
            for k in range(2):
                part = columns.at[j, first : first + half, k * width : (k + 1) * width]
                moves.append((ref.at[start + k * half : start + (k + 1) * half], part))
    copies = [
        pltpu.make_async_copy(ref, part, sems.at[n]) for n, (ref, part) in enumerate(moves)
    ]
    for copy in copies:
        copy.start()

    def summed(first):
        cols = slice(first, first + size)
        return kept[0, :, cols] + back[0, :, cols] + over[:, cols].astype(jnp.float32)

    def turned(values, gain):
        values = values * lax.rsqrt(jnp.mean(values * values, axis=-1, keepdims=True) + EPS) * gain
        other = jnp.where(
            low, pltpu.roll(values, size - size // 4, 1), pltpu.roll(values, size // 4, 1)
        )
        return (values * tables[0] + other * tables[1]).astype(jnp.bfloat16)

    for h in range(width // size):
        cols = slice(h * size, (h + 1) * size)
        query = turned(summed(h * size), gains[0:1])
        key = turned(summed(width + h * size), gains[1:2])
        value = summed(2 * width + h * size).astype(jnp.bfloat16)
        keys_out[:, cols] = key
        values_out[:, cols] = value
        keys = jnp.concatenate([key] + [s[:, cols] for s in (k_pair, k_x, k_d)], axis=0)
        seen = jnp.concatenate([value] + [s[:, cols] for s in (v_pair, v_x, v_d)], axis=0)
        scores = (
            lax.dot_general(
                query, keys, (((1,), (1,)), ((), ())), preferred_element_type=jnp.float32
            )
            * factor
        )
        weights = jnp.exp(scores - jnp.max(scores, axis=-1, keepdims=True))
        total = jnp.sum(weights, axis=-1, keepdims=True)
        product = jnp.dot(weights.astype(jnp.bfloat16), seen, preferred_element_type=jnp.float32)
        place = h * size // half
        start = h * size - place * half
        mixed[place, :, start : start + size] = (product / total).astype(jnp.bfloat16)

    for copy in copies:
        copy.wait()
    for j in range(4):
        one, two = (0, 1) if j < 2 else (rep, 1 - rep)
        term = jnp.dot(mixed[one], columns[j, :half], preferred_element_type=jnp.float32) + jnp.dot(
            mixed[two], columns[j, half:], preferred_element_type=jnp.float32
        )
        held[j ^ at[0]] = term.astype(jnp.bfloat16)
    near[0] = held[0]
    near[1] = held[2]
    far_one[...] = held[1]
    far_three[...] = held[3]


TIES = {'away0': ('far',),
 'cross_y': ('back0',),
 'kept0': ('o_pair',),
 'kept1': ('back0', 'back1', 'cross_far'),
 'last1': ('come1',),
 'norm1': ('far',),
 'one1': ('two1',),
 'pair1': ('away0',),
 's_pair': ('far',),
 'sent0': ('mine1', 'o_pair', 'one1', 's_pair'),
 'sent0_last': (),
 'turned1': ('o_y',)}
WORK = {'attend0': 6,
 'attend1': 9,
 'kept0': 10.5,
 'kept1': 10,
 'merge0': 10.6,
 'merge1': 9,
 'norm0': 10,
 'norm1': 11,
 'second': 6,
 'sent0': 9,
 'sent1': 9}


def cost(name):
    return pl.CostEstimate(flops=int(10 ** WORK[name]), bytes_accessed=10**6, transcendentals=0)


def params(mebibytes):
    return pltpu.CompilerParams(vmem_limit_bytes=mebibytes * 1024 * 1024)


def run_pack(timestep, latent, modulation):
    samples, rows, feats = latent.shape
    vmem = pl.BlockSpec(memory_space=pltpu.VMEM)
    return pl.pallas_call(
        pack_kernel,
        in_specs=[pl.BlockSpec(memory_space=pltpu.SMEM), vmem, vmem],
        out_specs=[vmem, vmem],
        out_shape=[
            jax.ShapeDtypeStruct((rows + 16, feats), jnp.bfloat16),
            jax.ShapeDtypeStruct((samples, feats), jnp.float32),
        ],
        compiler_params=params(16),
        name="pack",
    )(timestep, latent, modulation.transpose(1, 0, 2))


def second_kernel(latent, out):
    out[...] = latent[0]


def run_second(latent):
    _, rows, feats = latent.shape
    return pl.pallas_call(
        second_kernel,
        grid=(1,),
        in_specs=[pl.BlockSpec((1, rows, feats), lambda i: (1, 0, 0))],
        out_specs=pl.BlockSpec((rows, feats), lambda i: (0, 0)),
        out_shape=jax.ShapeDtypeStruct((rows, feats), jnp.bfloat16),
        compiler_params=params(16),
        cost_estimate=cost("second"),
        name="second",
    )(latent)


def run_norm(s, key, rows, blocks, turns):
    cols = blocks[0].shape[1]
    vmem = pl.BlockSpec(memory_space=pltpu.VMEM)
    shape = jax.ShapeDtypeStruct((rows, cols), jnp.bfloat16)
    return pl.pallas_call(
        functools.partial(norm_kernel, s),
        in_specs=[pl.BlockSpec(memory_space=pltpu.SMEM)] + [vmem] * 8,
        out_specs=[vmem] * 3,
        out_shape=[shape, shape, jax.ShapeDtypeStruct((2 * rows, cols), jnp.bfloat16)],
        scratch_shapes=[pltpu.VMEM((4, rows, cols), jnp.bfloat16)],
        compiler_params=params(16),
        cost_estimate=cost(f"norm{s}"),
        name="norm",
    )(key, *blocks, *turns)


def run_project(name, first, second, weight):
    rows, depth = first.shape
    wide = weight.shape[2]
    vmem = pl.BlockSpec((rows, depth), lambda i: (0, 0))
    return pl.pallas_call(
        project_kernel,
        grid=(3,),
        in_specs=[vmem] * 2 + [pl.BlockSpec((1, depth, wide), lambda i: (i, 0, 0))],
        out_specs=pl.BlockSpec((2, rows, wide), lambda i: (0, 0, i)),
        out_shape=jax.ShapeDtypeStruct((2, rows, 3 * wide), jnp.float32),
        scratch_shapes=[pltpu.VMEM((2 * rows, depth), jnp.bfloat16)],
        compiler_params=params(24),
        cost_estimate=cost(name),
        name="project",
    )(first, second, weight)


def run_merge(name, kept, back):
    _, rows, cols = kept.shape
    half = pl.BlockSpec((1, rows, cols), lambda i: (1, 0, 0))
    return pl.pallas_call(
        merge_kernel,
        grid=(1,),
        in_specs=[half, half],
        out_specs=pl.BlockSpec((rows, cols), lambda i: (0, 0)),
        out_shape=jax.ShapeDtypeStruct((rows, cols), jnp.bfloat16),
        compiler_params=params(16),
        cost_estimate=cost(name),
        name="merge",
    )(kept, back)


def run_attend(s, at, kept, back, over, stale, tables, gains, columns):
    rows, triple = over.shape
    width = triple // 3
    feats = columns[0].shape[1]
    full = pl.BlockSpec(memory_space=pltpu.VMEM)
    first = pl.BlockSpec((1, rows, triple), lambda i, at: (0, 0, 0))
    samples = 2
    seen = [
        pl.BlockSpec((rows, width), lambda i, at: (s, 0)),
        pl.BlockSpec((rows, width), lambda i, at: (samples + s, 0)),
    ]
    head = jax.ShapeDtypeStruct((rows, width), jnp.bfloat16)
    term = jax.ShapeDtypeStruct((rows, feats), jnp.bfloat16)
    return pl.pallas_call(
        attend_kernel,
        grid_spec=pltpu.PrefetchScalarGridSpec(
            num_scalar_prefetch=1,
            grid=(1,),
            in_specs=[first, first, full]
            + seen * 3
            + [full] * 2
            + [pl.BlockSpec(memory_space=pl.ANY)] * 6,
            out_specs=[full] * 5,
            scratch_shapes=[
                pltpu.VMEM((2, rows, width // 2), jnp.bfloat16),
                pltpu.VMEM((4, rows, feats), jnp.bfloat16),
                pltpu.VMEM((4, width, feats), jnp.bfloat16),
                pltpu.SemaphoreType.DMA((10,)),
            ],
        ),
        out_shape=[head, head, jax.ShapeDtypeStruct((2, rows, feats), jnp.bfloat16), term, term],
        compiler_params=params(28),
        cost_estimate=cost(f"attend{s}"),
        name="attend",
    )(at, kept, back, over, *[v for v in stale for _ in range(2)], tables, gains, *columns)


def shards_four(
    latent,
    timestep,
    positions,
    modulation,
    qkv_weight,
    out_weight,
    query_gain,
    key_gain,
    stale_keys,
    stale_values,
):
    samples, rows, part_width = latent.shape
    size = query_gain.shape[0]
    f = lax.axis_index("fsdp")
    z = lax.axis_index("patch")
    y = lax.axis_index("rep")

    def to_f(v, d):
        return lax.ppermute(v, "fsdp", [(i, i ^ d) for i in range(4)])

    def to_y(v):
        return lax.ppermute(v, "rep", [(0, 1), (1, 0)])

    def to_z(v, d):
        return lax.ppermute(v, "patch", [(i, i ^ d) for i in range(4)])

    def after(v, *deps):
        return lax.optimization_barrier((v, *deps))[0]

    made = {}

    def make(name, value):
        made[name] = value
        return value

    def tie(name, value):
        deps = [made[dep] for dep in TIES.get(name, ())]
        return after(value, *deps) if deps else value

    quarter = size // 4
    freq = 10000.0 ** (-jnp.arange(quarter, dtype=jnp.float32) / quarter)
    row_angle = (positions // GRID_W).astype(jnp.float32)[:, None] * freq
    col_angle = (positions % GRID_W).astype(jnp.float32)[:, None] * freq
    row_sin, col_sin = jnp.sin(row_angle), jnp.sin(col_angle)
    row_cos, col_cos = jnp.cos(row_angle), jnp.cos(col_angle)
    tables = jnp.stack(
        [
            jnp.concatenate([row_cos, row_cos, col_cos, col_cos], axis=-1),
            jnp.concatenate([-row_sin, row_sin, -col_sin, col_sin], axis=-1),
        ]
    )
    gains = jnp.stack([query_gain, key_gain])
    key = f ^ z
    at = jnp.stack([key, y]).astype(jnp.int32)

    weight = qkv_weight.transpose(1, 0, 2)
    packed, gate = run_pack(timestep, latent, modulation)
    make("packed", packed)
    two, one, three = [make("two0", to_z(packed, 2))], [make("one0", to_z(packed, 1))], []
    three.append(make("three0", to_z(two[0], 1)))
    deep = out_weight.shape[0] // 2
    width = stale_keys.shape[2]
    o_half = lax.dynamic_slice_in_dim(out_weight, y * deep, deep, 0)
    stale = [v.reshape(samples * rows, width) for v in (stale_keys, stale_values)]
    cut = len(stale) * samples * rows
    far = jnp.concatenate([*stale, o_half[:, :width], o_half[:, width:]])
    far = make("far", to_f(tie("far", far), 2))
    late = run_second(tie("late", latent))
    two.append(make("two1", to_z(late, 2)))
    one.append(make("one1", to_z(tie("one1", late), 1)))
    three.append(make("three1", to_z(two[1], 1)))
    turns = (packed, one[0], two[0], three[0])
    blocks = (turns, (late, one[1], two[1], three[1]))

    shared = []
    for s in range(samples):
        last = tie(f"norm{s}", blocks[s][3])
        mine, pair, away = run_norm(s, at, rows, (*blocks[s][:3], last), turns)
        make(f"mine{s}", mine)
        away = make(f"away{s}", to_f(tie(f"away{s}", away), 2))
        pair = make(f"pair{s}", to_f(tie(f"pair{s}", pair), 1))
        shared.append((mine, pair, away))
    o_y = make("o_y", to_y(tie("o_y", far[cut:])))
    o_pair = make("o_pair", to_f(tie("o_pair", out_weight), 1))
    s_pair = make("s_pair", to_f(tie("s_pair", jnp.concatenate(stale)), 1))
    cross_far = make("cross_far", to_f(tie("cross_far", far), 1))
    halves, turned = [], []
    for s in range(samples):
        mine, pair, away = shared[s]
        away = tie(f"use{s}", away)
        over, cross = away[:rows], make(f"cross{s}", to_f(tie(f"cross{s}", away[rows:]), 1))
        if s == 1:
            cross_y = make("cross_y", to_f(tie("cross_y", o_y), 1))
        if f"sent{s}_last" in TIES:
            kept = make(f"kept{s}", run_project(f"kept{s}", tie(f"kept{s}", mine), over, weight))
        sent = make(f"sent{s}", run_project(f"sent{s}", pair, tie(f"sent{s}", cross), weight))
        back = make(f"back{s}", to_f(tie(f"back{s}", sent), 1))
        if f"sent{s}_last" not in TIES:
            kept = make(f"kept{s}", run_project(f"kept{s}", tie(f"kept{s}", mine), over, weight))
        part = make(f"part{s}", run_merge(f"merge{s}", kept, back))
        halves.append((kept, back))
        turned.append(make(f"turned{s}", to_f(tie(f"turned{s}", part), 2)))
    columns = (out_weight, o_pair, far, o_y, cross_far, cross_y)
    stale_seen = (s_pair, far, cross_far)
    keys, values, outs = [], [], []
    for s in range(samples):
        kept, back = halves[s]
        new_keys, new_values, near, far_one, far_three = run_attend(
            s, at, kept, back, tie(f"attend{s}", turned[s]), stale_seen, tables, gains, columns
        )
        keys.append(new_keys)
        values.append(new_values)
        come = make(f"come{s}", to_z(far_three, 1))
        rest = near[1].astype(jnp.float32) + come.astype(jnp.float32)
        rest = make(f"rest{s}", to_z(rest.astype(jnp.bfloat16), 2))
        last = make(f"last{s}", to_z(tie(f"last{s}", far_one), 1))
        attended = (near[0].astype(jnp.float32) + last.astype(jnp.float32)) + rest.astype(jnp.float32)
        outs.append((latent[s].astype(jnp.float32) + gate[s] * attended).astype(jnp.bfloat16))
    return (jnp.stack(outs), jnp.stack(keys), jnp.stack(values))


def solution(mesh):
    in_specs = (
        P("rep", "fsdp", "patch"),
        P("rep"),
        P(("rep", "fsdp")),
        P(None, None, "patch"),
        P("fsdp", None, "patch"),
        P("patch", "fsdp"),
        P(),
        P(),
        P("rep", "fsdp", "patch"),
        P("rep", "fsdp", "patch"),
    )
    out_specs = (P("rep", "fsdp", "patch"), P("rep", "fsdp", "patch"), P("rep", "fsdp", "patch"))
    four = (mesh.shape["rep"], mesh.shape["fsdp"], mesh.shape["patch"]) == (2, 4, 4)
    step = shards_four if four else shards_any
    return jax.shard_map(step, mesh=mesh, in_specs=in_specs, out_specs=out_specs, check_vma=False)
```
